128 devices in a mesh: kv: 32 (over x, y, core), head: 4 (over z).
Axes of the slice: x: 4, y: 4, z: 4, core: 2. Of those that a mesh axis runs over, the one named last changes fastest.
Arguments:
- queries: bfloat16 [16, 128, 128], P(None, 'head'), may hold values from -200 to 200
- k_cache: bfloat16 [16, 2048, 8, 128], P(None, 'kv', 'head'), may hold values from -6 to 6
- v_cache: bfloat16 [16, 2048, 8, 128], P(None, 'kv', 'head'), may hold values from -6 to 6
- lengths: int32 [16], replicated, may hold values from 1 to 2048, 17408 in all
- residual_in: bfloat16 [16, 16384], replicated, may hold values from -60 to 60
- out_weight: bfloat16 [16384, 16384], P(('head', 'kv')), may hold values from -2 to 2
- norm_gain: bfloat16 [16384], replicated, may hold values from 0.099609375 to 1.8984375
- gate_weight: bfloat16 [26624, 16384], P(('kv', 'head')), may hold values from -0.046875 to 0.046875
- up_weight: bfloat16 [26624, 16384], P(('kv', 'head')), may hold values from -0.046875 to 0.046875
- down_weight: bfloat16 [26624, 16384], P(('kv', 'head')), may hold values from -0.125 to 0.125
Outputs:
- mixed: bfloat16 [16, 16384], P(None, ('kv', 'head'))
The draws below stay inside these ranges and needn't reach their ends.
All inputs are finite; a program needn't handle non-finite values.
Results may differ from the reference program's by a relative error of at most 0.015.
Values may be sent and summed in bfloat16 or wider, within the bound.
No kernel may reach another device: no remote copies, remote signals or barrier semaphores. Data moves between devices by JAX's collectives and lax.ppermute only.
A program may use at most 128 MiB of HBM per device.

```python
import math
import jax
import jax.numpy as jnp
import numpy as np
from jax import lax

D = 16384
HEAD_DIM = 128
KV_HEADS = 8
FF = 26624
ROWS = 16
S_DEV = 64
HEADS = 128
CTX = 2048
N_KV = 32


def shared_keys(key):
    return jnp.clip(jax.random.normal(key, (ROWS, CTX, KV_HEADS, HEAD_DIM), jnp.float32), -6.0, 6.0)


def draw_k_cache(key, part):
    shared = shared_keys(key)
    return shared.astype(jnp.bfloat16)


def draw_queries(key, part):
    key = jax.random.fold_in(key, 5)
    values = jax.random.normal(key, (ROWS, HEADS, HEAD_DIM), jnp.float32)
    return jnp.clip(values, -200.0, 200.0).astype(jnp.bfloat16)


def draw_residual_in(key, part):
    key = jax.random.fold_in(key, 7)
    pieces = jax.random.split(key, 3)
    row_scale = jnp.exp(jax.random.uniform(pieces[0], (ROWS, 1), jnp.float32, 0.0, math.log(10.0)))
    column_scale = jnp.exp(jax.random.uniform(pieces[1], (1, D), jnp.float32, 0.0, math.log(10.0)))
    values = jnp.clip(jax.random.normal(pieces[2], (ROWS, D), jnp.float32), -4.0, 4.0) * row_scale * column_scale * 0.1
    return jnp.clip(values, -60.0, 60.0).astype(jnp.bfloat16)


def spiked(entries, stream_key, source, target, parts, factor):
    owner, partner = [(jnp.arange(entries.shape[dim]) // (entries.shape[dim] // parts)).reshape([-1 if axis == dim else 1 for axis in range(entries.ndim)]) for dim in (source, target)]
    chosen = jax.random.permutation(stream_key, parts)[partner]
    strong = (owner == chosen) | (owner == (partner + parts // 2) % parts)
    return jnp.where(strong, factor * entries, entries)


def shard_levels(key, dims, cuts, smallest, high):
    factor_of = 1.0
    for position, blocks in cuts:
        steps = jax.random.uniform(jax.random.fold_in(jax.random.fold_in(key, 6), position), (blocks,), jnp.float32, smallest / len(cuts), high / len(cuts))
        factor_of = factor_of * jnp.repeat(jnp.exp(steps), dims[position] // blocks).reshape((-1,) + (1,) * (len(dims) - 1 - position))
    return factor_of


def split_up(number_of, total, most, lean):
    weights = [(1 << 20) // math.isqrt(standing ** lean) + 1 for standing in range(2, number_of + 1)]
    rest, counts = total - most - (number_of - 1), [1] * (number_of - 1)
    while rest > 0:
        free = [i for i in range(number_of - 1) if counts[i] < most]
        whole, remaining = sum([weights[i] for i in free]), rest
        for i in free:
            addition = min(most - counts[i], max(1, remaining * weights[i] // whole), rest)
            counts[i] = counts[i] + addition
            rest = rest - addition
    return np.array([most] + counts)


def uneven_parts(stream_key, count, total, most, slope):
    if count == 2:
        one = jax.random.randint(stream_key, (), max(1, total - most), min(most, total - 1) + 1)
        return jnp.stack([one, total - one])
    sizes = jnp.asarray(split_up(count, total, most, slope), jnp.int32)
    twos = (count - 1) // 2
    source_of, receiver = sizes[1:1 + 2 * twos:2], sizes[2:2 + 2 * twos:2]
    margin = jnp.minimum(source_of - 1, most - receiver)
    passed = jax.random.randint(jax.random.fold_in(stream_key, 1), (twos,), 0, 1 << 20) % (margin + 1)
    sizes = sizes.at[1:1 + 2 * twos:2].set(source_of - passed).at[2:2 + 2 * twos:2].set(receiver + passed)
    return sizes[jax.random.permutation(jax.random.fold_in(stream_key, 2), count)]


def noise(stream_key, extent, deviation, most, cuts=(), kind=jnp.bfloat16):
    values = jax.random.normal(stream_key, extent, jnp.float32) * deviation
    if len(cuts) > 0:
        values = shard_levels(stream_key, extent, cuts, -0.22, 0.18) * values
    return jnp.clip(values, min=-most, max=most).astype(kind)


def bell_draw_with(key, dims, width, reach, cuts, heavy, kind=jnp.bfloat16):
    array = width * jax.random.normal(key, dims, jnp.float32)
    if cuts:
        array = array * shard_levels(key, dims, cuts, -0.22, 0.18)
    return jnp.clip(spiked(array, jax.random.fold_in(key, 3), *heavy), -reach, reach).astype(kind)


def setup_inputs(seed: int = 0) -> dict:
    splits = jax.random.split(jax.random.key(seed), 11)
    return {
        "queries": draw_queries(jax.random.fold_in(splits[10], 71), 0),
        "k_cache": draw_k_cache(jax.random.fold_in(splits[10], 71), 0),
        "v_cache": noise(splits[2], (ROWS, CTX, KV_HEADS, HEAD_DIM), 1.0, 6.0, ((1, 32), (2, 4))),
        "lengths": uneven_parts(splits[3], ROWS, (ROWS + 1) * CTX // 2, CTX, 2).astype(jnp.int32),
        "residual_in": draw_residual_in(jax.random.fold_in(splits[10], 71), 0),
        "out_weight": bell_draw_with(splits[5], (HEADS * HEAD_DIM, D), HEAD_DIM ** -0.5, 2.0, ((0, 128),), (0, 1, 128, 5.5)),
        "norm_gain": jnp.clip(1.0 + 0.18 * jax.random.normal(splits[6], (D,), jnp.float32), 0.099609375, 1.8984375).astype(jnp.bfloat16),
        "gate_weight": noise(splits[7], (FF, D), D ** -0.5, 0.046875, ((0, 128),)),
        "up_weight": noise(splits[8], (FF, D), D ** -0.5, 0.046875, ((0, 128),)),
        "down_weight": bell_draw_with(splits[9], (FF, D), FF ** -0.5, 0.125, ((0, 128),), (0, 1, 128, 5.5)),
    }


def reference(queries, k_cache, v_cache, lengths, residual_in, out_weight, norm_gain, gate_weight, up_weight, down_weight):
    group_size = HEADS // KV_HEADS
    slots = jnp.arange(CTX, dtype=jnp.int32)
    live = (slots[None, :] < lengths[:, None]).reshape(ROWS, 1, 1, N_KV, S_DEV)
    query_groups = queries.astype(jnp.float32).reshape(ROWS, KV_HEADS, group_size, HEAD_DIM)
    scores = jnp.einsum('bkgd,bskd->bkgs', query_groups, k_cache.astype(jnp.float32)) * HEAD_DIM ** (-0.5)
    scores = scores.reshape(ROWS, KV_HEADS, group_size, N_KV, S_DEV)
    masked = jnp.where(live, scores, -1e+30)
    block_max = lax.optimization_barrier(jnp.max(masked, axis=-1))
    weights = jnp.where(live, jnp.exp(masked - block_max[..., None]), 0.0)
    block_total = lax.optimization_barrier(jnp.sum(weights, axis=-1))
    values = v_cache.astype(jnp.float32).reshape(ROWS, N_KV, S_DEV, KV_HEADS, HEAD_DIM)
    rounded = weights.astype(jnp.bfloat16).astype(jnp.float32)
    block_out = jnp.einsum('bkgns,bnskd->bkgnd', rounded, values)
    top = lax.optimization_barrier(jnp.max(block_max, axis=-1))
    scale = jnp.exp(block_max - top[..., None])
    total = lax.optimization_barrier(jnp.sum(scale * block_total, axis=-1))
    merged = lax.optimization_barrier(jnp.sum(scale[..., None] * block_out, axis=-2))
    attended = (merged / total[..., None]).reshape(ROWS, HEADS * HEAD_DIM).astype(jnp.bfloat16)
    stream = residual_in.astype(jnp.float32) + jnp.dot(attended, out_weight, preferred_element_type=jnp.float32)
    factor = lax.rsqrt(lax.optimization_barrier(jnp.mean(stream * stream, axis=1, keepdims=True)) + 1e-05)
    normed = (stream * factor * norm_gain.astype(jnp.float32)).astype(jnp.bfloat16)
    gate = jnp.dot(normed, gate_weight.T, preferred_element_type=jnp.float32)
    upward = jnp.dot(normed, up_weight.T, preferred_element_type=jnp.float32)
    hidden = (jax.nn.silu(gate) * upward).astype(jnp.bfloat16)
    return (stream + jnp.dot(hidden, down_weight, preferred_element_type=jnp.float32)).astype(jnp.bfloat16)
```

```python
import jax
import jax.numpy as jnp
from jax import lax
from jax.sharding import Mesh, PartitionSpec as P

XY = ("x", "y")
KV = ("x", "y", "c")
ALL = ("x", "y", "c", "z")


def attention_message(queries, k_cache, v_cache, lengths):
    rows, heads, width = queries.shape
    span, groups = k_cache.shape[1], k_cache.shape[2]
    size = heads // groups
    positions = lax.axis_index(KV) * span + jnp.arange(span, dtype=jnp.int32)
    live = (positions[None, :] < lengths[:, None])[:, None, None, :]
    grouped = queries.reshape(rows, groups, size, width)
    scores = jnp.einsum(
        "bkgd,bskd->bkgs", grouped, k_cache, preferred_element_type=jnp.float32
    ) * width ** (-0.5)
    masked = jnp.where(live, scores, -1e30)
    point = jnp.max(masked, axis=-1).astype(jnp.bfloat16)
    weights = jnp.where(live, jnp.exp(masked - point.astype(jnp.float32)[..., None]), 0.0)
    total = jnp.sum(weights, axis=-1)
    out = jnp.einsum(
        "bkgs,bskd->bkgd", weights.astype(jnp.bfloat16), v_cache, preferred_element_type=jnp.float32
    )
    out = out.reshape(rows, heads, width).astype(jnp.bfloat16)
    stats = jnp.concatenate(
        [
            jnp.broadcast_to(a.reshape(rows, heads, 1).astype(jnp.bfloat16), (rows, heads, width // 2))
            for a in (point, total)
        ],
        axis=2,
    )
    return jnp.concatenate([out, stats], axis=0).transpose(1, 0, 2)


def merge(came, rows):
    out = came[:, :rows].astype(jnp.float32)
    width = out.shape[2]
    point = came[:, rows:, :1].astype(jnp.float32)
    total = came[:, rows:, width // 2 : width // 2 + 1].astype(jnp.float32)
    scale = jnp.exp(point - jnp.max(point, axis=0, keepdims=True))
    return jnp.sum(scale * out, axis=0) / jnp.sum(scale * total, axis=0)


def exchange(block, axis, flip):
    size = lax.axis_size(axis)
    return lax.ppermute(block, axis, [(i, i ^ flip) for i in range(size)])


def per_device(
    queries, k_cache, v_cache, lengths, residual_in, out_weight, norm_gain, gate_weight, up_weight, down_weight
):
    rows = queries.shape[0]
    width = residual_in.shape[1]
    message = attention_message(queries, k_cache, v_cache, lengths)
    came = lax.all_to_all(message, KV, split_axis=0, concat_axis=0, tiled=True)
    attended = merge(came, rows).astype(jnp.bfloat16)
    planes = lax.axis_size(XY)
    chunk = width // planes
    projected = jnp.dot(attended, out_weight, preferred_element_type=jnp.float32)
    pieces = projected.astype(jnp.bfloat16).reshape(rows, planes, chunk).transpose(1, 0, 2)
    pieces = lax.all_to_all(pieces, XY, split_axis=0, concat_axis=0, tiled=True)
    part = jnp.sum(pieces.astype(jnp.float32), axis=0)
    part = part + exchange(part, "c", 1)
    part = part + exchange(part, "z", 1)
    part = part + exchange(part, "z", 3)
    plane = lax.axis_index(XY)
    stream = part + lax.dynamic_slice_in_dim(residual_in, plane * chunk, chunk, 1).astype(jnp.float32)
    sent = jnp.broadcast_to(stream.astype(jnp.bfloat16)[None], (planes, rows, chunk))
    whole = lax.all_to_all(sent, XY, split_axis=0, concat_axis=0, tiled=True)
    whole = whole.transpose(1, 0, 2).reshape(rows, width).astype(jnp.float32)
    factor = lax.rsqrt(jnp.mean(whole * whole, axis=1, keepdims=True) + 1e-05)
    normed = (whole * factor * norm_gain.astype(jnp.float32)).astype(jnp.bfloat16)
    gate = jnp.einsum("bd,fd->bf", normed, gate_weight, preferred_element_type=jnp.float32)
    upward = jnp.einsum("bd,fd->bf", normed, up_weight, preferred_element_type=jnp.float32)
    hidden = (jax.nn.silu(gate) * upward).astype(jnp.bfloat16)
    devices = lax.axis_size(ALL)
    share = width // devices
    down = jnp.dot(hidden, down_weight, preferred_element_type=jnp.float32)
    down = down.astype(jnp.bfloat16).reshape(rows, devices, share).transpose(1, 0, 2)
    down = lax.all_to_all(down, ALL, split_axis=0, concat_axis=0, tiled=True)
    down = jnp.sum(down.astype(jnp.float32), axis=0)
    own = lax.dynamic_slice_in_dim(stream, lax.axis_index(("c", "z")) * share, share, 1)
    return (own + down).astype(jnp.bfloat16)


def solution(mesh):
    fine = Mesh(mesh.devices.reshape(4, 4, 2, 4), ALL)
    placed = (
        P(None, "z", None),
        P(None, KV, "z", None),
        P(None, KV, "z", None),
        P(),
        P(),
        P(("z",) + KV, None),
        P(),
        P(ALL, None),
        P(ALL, None),
        P(ALL, None),
    )
    return jax.shard_map(per_device, mesh=fine, in_specs=placed, out_specs=P(None, ALL), check_vma=False)
```

```python
import functools

import jax
import jax.numpy as jnp
from jax import lax
from jax.experimental import pallas as pl
from jax.experimental.pallas import tpu as pltpu
from jax.sharding import Mesh, PartitionSpec as P

KV = ("x", "y", "c")
ALL = ("x", "y", "c", "z")
LANES = 128
MIB = 2**20
LAST = (((1,), (1,)), ((), ()))
FIRST = (((0,), (0,)), ((), ()))


def flat_index(axes):
    index = 0
    for axis in axes:
        index = index * lax.axis_size(axis) + lax.axis_index(axis)
    return index


def call(kernel, outs, args, spaces, scratch=(), limit=16 * MIB, flops=0):
    shapes = [jax.ShapeDtypeStruct(*out) for out in outs]
    specs = [pl.BlockSpec(memory_space=pltpu.VMEM)] * len(outs)
    return pl.pallas_call(
        kernel,
        out_shape=shapes,
        in_specs=[pl.BlockSpec(memory_space=space) for space in spaces],
        out_specs=specs,
        scratch_shapes=list(scratch),
        compiler_params=pltpu.CompilerParams(vmem_limit_bytes=limit),
        cost_estimate=pl.CostEstimate(flops=flops, bytes_accessed=MIB, transcendentals=0),
    )(*args)


def attention_kernel(
    groups,
    lengths_hbm,
    q_hbm,
    k_hbm,
    v_hbm,
    weight_hbm,
    residual_hbm,
    message_ref,
    weight_ref,
    residual_ref,
    lengths_ref,
    q_ref,
    k_ref,
    v_ref,
    held,
    sems,
):
    rows, heads, width = q_ref.shape
    slots = k_ref.shape[1]
    span = slots // groups
    size = heads // groups
    height = message_ref.shape[1]
    columns = pl.ds(pl.multiple_of(flat_index(ALL) * LANES, LANES), LANES)
    loads = [
        pltpu.make_async_copy(source, target, sems.at[i])
        for i, (source, target) in enumerate(
            (
                (q_hbm, q_ref),
                (k_hbm, k_ref),
                (lengths_hbm, lengths_ref),
                (v_hbm, v_ref),
                (weight_hbm, weight_ref),
                (residual_hbm.at[:, columns], residual_ref),
            )
        )
    ]
    for load in loads:
        load.start()
    base = flat_index(KV) * span
    head = lax.broadcasted_iota(jnp.int32, (heads, slots), 0)
    slot = lax.broadcasted_iota(jnp.int32, (heads, slots), 1)
    own = (head // size) == (slot % groups)
    position = jnp.where(own, base + slot // groups, jnp.int32(2**30))
    lane = lax.broadcasted_iota(jnp.int32, (heads, width), 1)
    half = width // 2
    for load in loads[:3]:
        load.wait()
    scores = [
        lax.dot_general(q_ref[b], k_ref[b], LAST, preferred_element_type=jnp.float32) * width ** (-0.5)
        for b in range(rows)
    ]
    weights, packed = [], []
    for b in range(rows):
        live = position < lengths_ref[b]
        masked = jnp.where(live, scores[b], -1e30)
        point = jnp.max(masked, axis=1, keepdims=True).astype(jnp.bfloat16).astype(jnp.float32)
        weight = jnp.where(live, jnp.exp(masked - point), 0.0)
        weights.append(weight.astype(jnp.bfloat16))
        packed.append((point, jnp.sum(weight, axis=1, keepdims=True)))
    loads[3].wait()
    outs = [jnp.dot(weights[b], v_ref[b], preferred_element_type=jnp.float32) for b in range(rows)]
    for b in range(rows):
        held[pl.ds(b, heads, stride=height), :] = outs[b]
    for b in range(rows // 2):
        (point, total), (later_point, later_total) = packed[b], packed[b + rows // 2]
        stats = jnp.where(
            lane < half,
            jnp.where(lane < half // 2, point, total),
            jnp.where(lane < half + half // 2, later_point, later_total),
        )
        held[pl.ds(rows + b, heads, stride=height), :] = stats
    for h in range(heads):
        message_ref[h] = held[h * height : (h + 1) * height, :].astype(jnp.bfloat16)
    loads[4].wait()
    loads[5].wait()


def attention(lengths, queries, k_cache, v_cache, weight, residual):
    rows, heads, width = queries.shape
    span, groups = k_cache.shape[1:3]
    height = rows + rows // 2
    cache = (rows, span * groups, width)
    return call(
        functools.partial(attention_kernel, groups),
        [
            ((heads, height, width), jnp.bfloat16),
            (weight.shape, jnp.bfloat16),
            ((rows, LANES), jnp.bfloat16),
        ],
        [
            pltpu.with_memory_space_constraint(a, pltpu.HBM)
            for a in (lengths, queries, k_cache.reshape(cache), v_cache.reshape(cache), weight, residual)
        ],
        [pltpu.HBM] * 6,
        [
            pltpu.SMEM(lengths.shape, jnp.int32),
            pltpu.VMEM(queries.shape, jnp.bfloat16),
            pltpu.VMEM(cache, jnp.bfloat16),
            pltpu.VMEM(cache, jnp.bfloat16),
            pltpu.VMEM((heads * height, width), jnp.float32),
            pltpu.SemaphoreType.DMA((6,)),
        ],
        limit=12 * MIB,
    )


def project_kernel(rows, step, came_ref, weight_ref, out_ref):
    parts, _, width = came_ref.shape
    half = width // 2
    stats = came_ref[:, rows:, :].astype(jnp.float32)
    point = jnp.concatenate([stats[:, :, :1], stats[:, :, half : half + 1]], axis=1)
    quarter = half // 2
    total = jnp.concatenate(
        [stats[:, :, quarter : quarter + 1], stats[:, :, half + quarter : half + quarter + 1]], axis=1
    )
    scale = jnp.exp(point - jnp.max(point, axis=0, keepdims=True))
    out = jnp.sum(scale * came_ref[:, :rows, :].astype(jnp.float32), axis=0)
    attended = (out / jnp.sum(scale * total, axis=0)).astype(jnp.bfloat16)
    for at in range(0, weight_ref.shape[1], step):
        product = jnp.dot(attended, weight_ref[:, at : at + step], preferred_element_type=jnp.float32)
        for j in range(step // LANES):
            out_ref[at // LANES + j] = product[:, j * LANES : (j + 1) * LANES].astype(jnp.bfloat16)


def project(came, weight, rows, step=2048):
    pieces = weight.shape[1] // LANES
    return call(
        functools.partial(project_kernel, rows, step),
        [((pieces, rows, LANES), jnp.bfloat16)],
        [came, weight],
        [pltpu.VMEM] * 2,
        limit=12 * MIB,
        flops=10**10,
    )[0]


def stream_kernel(came_ref, residual_ref, stream_ref, sent_ref):
    total = jnp.sum(came_ref[...].astype(jnp.float32), axis=0)
    stream = total + residual_ref[...].astype(jnp.float32)
    stream_ref[...] = stream
    sent_ref[...] = jnp.broadcast_to(stream.astype(jnp.bfloat16)[None], sent_ref.shape)


def stream_sum(came, residual):
    shape = came.shape
    return call(
        stream_kernel,
        [(shape[1:], jnp.float32), (shape, jnp.bfloat16)],
        [came, residual],
        [pltpu.VMEM] * 2,
    )


def feed_forward_kernel(step, whole_ref, gain_ref, gate_ref, up_ref, down_ref, out_ref):
    pieces, rows, _ = whole_ref.shape
    units, width = gate_ref.shape
    per = step // LANES
    gate = jnp.zeros((units, rows), jnp.float32)
    up = jnp.zeros((units, rows), jnp.float32)
    square = jnp.zeros((rows, LANES), jnp.float32)
    for k in range(width // step):
        parts = []
        for j in range(k * per, (k + 1) * per):
            part = whole_ref[j].astype(jnp.float32)
            square += part * part
            parts.append((part * gain_ref[j : j + 1, :].astype(jnp.float32)).astype(jnp.bfloat16))
        block = jnp.concatenate(parts, axis=1)
        columns = slice(k * step, (k + 1) * step)
        gate += lax.dot_general(gate_ref[:, columns], block, LAST, preferred_element_type=jnp.float32)
        up += lax.dot_general(up_ref[:, columns], block, LAST, preferred_element_type=jnp.float32)
    factor = lax.rsqrt(jnp.sum(square.T, axis=0, keepdims=True) * (1.0 / width) + 1e-05)
    gate = gate * factor
    hidden = (gate / (1.0 + jnp.exp(-gate)) * (up * factor)).T.astype(jnp.bfloat16)
    for k in range(width // step):
        product = jnp.dot(hidden, down_ref[:, k * step : (k + 1) * step], preferred_element_type=jnp.float32)
        for j in range(per):
            out_ref[k * per + j] = product[:, j * LANES : (j + 1) * LANES].astype(jnp.bfloat16)


def feed_forward(whole, gain, gate, up, down, step=2048):
    return call(
        functools.partial(feed_forward_kernel, step),
        [(whole.shape, jnp.bfloat16)],
        [whole, gain.reshape(-1, LANES), gate, up, down],
        [pltpu.VMEM] * 5,
        limit=30 * MIB,
    )[0]


def swap(blocks, axes):
    return lax.all_to_all(blocks, axes, split_axis=0, concat_axis=0, tiled=True)


def per_device(
    queries, k_cache, v_cache, lengths, residual_in, out_weight, norm_gain, gate_weight, up_weight, down_weight
):
    rows = queries.shape[0]
    message, weight, residual = attention(lengths, queries, k_cache, v_cache, out_weight, residual_in)
    came = swap(message, KV)
    stream, sent = stream_sum(swap(project(came, weight, rows), ALL), residual)
    whole = swap(sent, ALL)
    down = swap(feed_forward(whole, norm_gain, gate_weight, up_weight, down_weight), ALL)
    return (stream + jnp.sum(down.astype(jnp.float32), axis=0)).astype(jnp.bfloat16)


def solution(mesh):
    fine = Mesh(mesh.devices.reshape(4, 4, 2, 4), ALL)
    placed = (
        P(None, "z", None),
        P(None, KV, "z", None),
        P(None, KV, "z", None),
        P(),
        P(),
        P(("z",) + KV, None),
        P(),
        P(ALL, None),
        P(ALL, None),
        P(ALL, None),
    )
    return jax.shard_map(per_device, mesh=fine, in_specs=placed, out_specs=P(None, ALL), check_vma=False)
```

```python
import functools

import jax
import jax.numpy as jnp
from jax import lax
from jax.experimental import pallas as pl
from jax.experimental.pallas import tpu as pltpu
from jax.sharding import Mesh, PartitionSpec as P

KV = ("x", "y", "c")
ALL = ("x", "y", "c", "z")
CHIPS = ("x", "y", "z")
LANES = 128
MIB = 2**20
LAST = (((1,), (1,)), ((), ()))


def flat_index(axes):
    index = 0
    for axis in axes:
        index = index * lax.axis_size(axis) + lax.axis_index(axis)
    return index


def call(kernel, outs, args, spaces, scratch=(), limit=16 * MIB, flops=0):
    shapes = [jax.ShapeDtypeStruct(*out) for out in outs]
    specs = [pl.BlockSpec(memory_space=pltpu.VMEM)] * len(outs)
    return pl.pallas_call(
        kernel,
        out_shape=shapes,
        in_specs=[pl.BlockSpec(memory_space=space) for space in spaces],
        out_specs=specs,
        scratch_shapes=list(scratch),
        compiler_params=pltpu.CompilerParams(vmem_limit_bytes=limit),
        cost_estimate=pl.CostEstimate(flops=flops, bytes_accessed=MIB, transcendentals=0),
    )(*args)


def attention_kernel(
    groups,
    lengths_hbm,
    q_hbm,
    k_hbm,
    v_hbm,
    weight_hbm,
    residual_hbm,
    message_ref,
    weight_ref,
    residual_ref,
    lengths_ref,
    q_ref,
    k_ref,
    v_ref,
    held,
    sems,
):
    rows, heads, width = q_ref.shape
    slots = k_ref.shape[1]
    span = slots // groups
    size = heads // groups
    height = message_ref.shape[1]
    columns = pl.ds(pl.multiple_of(flat_index(ALL) * LANES, LANES), LANES)
    loads = [
        pltpu.make_async_copy(source, target, sems.at[i])
        for i, (source, target) in enumerate(
            (
                (q_hbm, q_ref),
                (k_hbm, k_ref),
                (lengths_hbm, lengths_ref),
                (v_hbm, v_ref),
                (weight_hbm, weight_ref),
                (residual_hbm.at[:, columns], residual_ref),
            )
        )
    ]
    for load in loads:
        load.start()
    base = flat_index(KV) * span
    head = lax.broadcasted_iota(jnp.int32, (heads, slots), 0)
    slot = lax.broadcasted_iota(jnp.int32, (heads, slots), 1)
    own = (head // size) == (slot % groups)
    position = jnp.where(own, base + slot // groups, jnp.int32(2**30))
    lane = lax.broadcasted_iota(jnp.int32, (heads, width), 1)
    half = width // 2
    for load in loads[:3]:
        load.wait()
    scores = [
        lax.dot_general(q_ref[b], k_ref[b], LAST, preferred_element_type=jnp.float32) * width ** (-0.5)
        for b in range(rows)
    ]
    weights, packed = [], []
    for b in range(rows):
        live = position < lengths_ref[b]
        masked = jnp.where(live, scores[b], -1e30)
        point = jnp.max(masked, axis=1, keepdims=True).astype(jnp.bfloat16).astype(jnp.float32)
        weight = jnp.where(live, jnp.exp(masked - point), 0.0)
        weights.append(weight.astype(jnp.bfloat16))
        packed.append((point, jnp.sum(weight, axis=1, keepdims=True)))
    loads[3].wait()
    outs = [jnp.dot(weights[b], v_ref[b], preferred_element_type=jnp.float32) for b in range(rows)]
    for b in range(rows):
        held[pl.ds(b, heads, stride=height), :] = outs[b]
    for b in range(rows // 2):
        (point, total), (later_point, later_total) = packed[b], packed[b + rows // 2]
        stats = jnp.where(
            lane < half,
            jnp.where(lane < half // 2, point, total),
            jnp.where(lane < half + half // 2, later_point, later_total),
        )
        held[pl.ds(rows + b, heads, stride=height), :] = stats
    for h in range(heads):
        message_ref[h] = held[h * height : (h + 1) * height, :].astype(jnp.bfloat16)
    loads[4].wait()
    loads[5].wait()


def attention(lengths, queries, k_cache, v_cache, weight, residual):
    rows, heads, width = queries.shape
    span, groups = k_cache.shape[1:3]
    height = rows + rows // 2
    cache = (rows, span * groups, width)
    return call(
        functools.partial(attention_kernel, groups),
        [
            ((heads, height, width), jnp.bfloat16),
            (weight.shape, jnp.bfloat16),
            ((rows, LANES), jnp.bfloat16),
        ],
        [
            pltpu.with_memory_space_constraint(a, pltpu.HBM)
            for a in (lengths, queries, k_cache.reshape(cache), v_cache.reshape(cache), weight, residual)
        ],
        [pltpu.HBM] * 6,
        [
            pltpu.SMEM(lengths.shape, jnp.int32),
            pltpu.VMEM(queries.shape, jnp.bfloat16),
            pltpu.VMEM(cache, jnp.bfloat16),
            pltpu.VMEM(cache, jnp.bfloat16),
            pltpu.VMEM((heads * height, width), jnp.float32),
            pltpu.SemaphoreType.DMA((6,)),
        ],
        limit=12 * MIB,
    )


def columns_of(piece, side, run):
    return pl.ds(pl.multiple_of((2 * piece + side) * run, run), run)


def other_core():
    return 1 - lax.axis_index("c")


def half_product(left, weight_ref, side, out_ref):
    per = lax.axis_size("z")
    run = per * LANES
    for piece in range(out_ref.shape[0] // per):
        product = jnp.dot(left, weight_ref[:, columns_of(piece, side, run)], preferred_element_type=jnp.float32)
        for j in range(per):
            out_ref[piece * per + j] = product[:, j * LANES : (j + 1) * LANES].astype(out_ref.dtype)


def merge_kernel(rows, came_ref, weight_ref, sent_ref, attended_ref):
    width = came_ref.shape[2]
    half = width // 2
    stats = came_ref[:, rows:, :].astype(jnp.float32)
    point = jnp.concatenate([stats[:, :, :1], stats[:, :, half : half + 1]], axis=1)
    quarter = half // 2
    total = jnp.concatenate(
        [stats[:, :, quarter : quarter + 1], stats[:, :, half + quarter : half + quarter + 1]], axis=1
    )
    scale = jnp.exp(point - jnp.max(point, axis=0, keepdims=True))
    out = jnp.sum(scale * came_ref[:, :rows, :].astype(jnp.float32), axis=0)
    attended = (out / jnp.sum(scale * total, axis=0)).astype(jnp.bfloat16)
    attended_ref[...] = attended
    half_product(attended, weight_ref, other_core(), sent_ref)


def merge_and_project(came, weight, rows):
    chips = weight.shape[1] // LANES // 2
    return call(
        functools.partial(merge_kernel, rows),
        [((chips, rows, LANES), jnp.bfloat16), ((rows, came.shape[2]), jnp.bfloat16)],
        [came, weight],
        [pltpu.VMEM] * 2,
        limit=12 * MIB,
        flops=10**10,
    )


def own_kernel(left_ref, weight_ref, out_ref):
    half_product(left_ref[...], weight_ref, lax.axis_index("c"), out_ref)


def own_half(left, weight):
    chips = weight.shape[1] // LANES // 2
    return call(
        own_kernel,
        [((chips, left.shape[0], LANES), jnp.float32)],
        [left, weight],
        [pltpu.VMEM] * 2,
        limit=12 * MIB,
        flops=10**9,
    )[0]


def add_kernel(own_ref, came_ref, out_ref):
    out_ref[...] = (own_ref[...] + came_ref[...].astype(jnp.float32)).astype(jnp.bfloat16)


def add(own, came):
    return call(add_kernel, [(came.shape, jnp.bfloat16)], [own, came], [pltpu.VMEM] * 2)[0]


def stream_kernel(came_ref, residual_ref, stream_ref, sent_ref):
    total = jnp.sum(came_ref[...].astype(jnp.float32), axis=0)
    stream = total + residual_ref[...].astype(jnp.float32)
    stream_ref[...] = stream
    sent_ref[...] = jnp.broadcast_to(stream.astype(jnp.bfloat16)[None], sent_ref.shape)


def stream_sum(came, residual):
    shape = came.shape
    return call(
        stream_kernel,
        [(shape[1:], jnp.float32), (shape, jnp.bfloat16)],
        [came, residual],
        [pltpu.VMEM] * 2,
    )


def gate_up(side, whole_ref, gain_ref, gate_ref, up_ref, gate, up, square):
    per = lax.axis_size("z")
    run = per * LANES
    for piece in range(whole_ref.shape[0] // per):
        parts = []
        for j in range(per):
            part = whole_ref[piece * per + j].astype(jnp.float32)
            square += part * part
            gain = gain_ref[pl.ds((2 * piece + side) * per + j, 1), :]
            parts.append((part * gain).astype(jnp.bfloat16))
        block = jnp.concatenate(parts, axis=1)
        columns = columns_of(piece, side, run)
        gate += lax.dot_general(gate_ref[:, columns], block, LAST, preferred_element_type=jnp.float32)
        up += lax.dot_general(up_ref[:, columns], block, LAST, preferred_element_type=jnp.float32)
    return gate, up, square


def first_kernel(whole_ref, gain_ref, gate_ref, up_ref, gate_out, up_out, square_out):
    zeros = jnp.zeros(gate_out.shape, jnp.float32)
    gate_out[...], up_out[...], square_out[...] = gate_up(
        lax.axis_index("c"), whole_ref, gain_ref, gate_ref, up_ref, zeros, zeros, jnp.zeros(square_out.shape, jnp.float32)
    )


def first_half(whole, gain, gate, up):
    rows, units = whole.shape[1], gate.shape[0]
    return call(
        first_kernel,
        [((units, rows), jnp.float32), ((units, rows), jnp.float32), ((rows, LANES), jnp.float32)],
        [whole, gain, gate, up],
        [pltpu.VMEM] * 4,
        limit=24 * MIB,
        flops=10**9,
    )


def second_kernel(
    whole_ref, gain_ref, gate_ref, up_ref, down_ref, gate_sum, up_sum, square_sum, sent_ref, hidden_ref
):
    gate, up, square = gate_up(
        other_core(), whole_ref, gain_ref, gate_ref, up_ref, gate_sum[...], up_sum[...], square_sum[...]
    )
    width = gate_ref.shape[1]
    factor = lax.rsqrt(jnp.sum(square.T, axis=0, keepdims=True) * (1.0 / width) + 1e-05)
    gate = gate * factor
    hidden = (gate / (1.0 + jnp.exp(-gate)) * (up * factor)).T.astype(jnp.bfloat16)
    hidden_ref[...] = hidden
    half_product(hidden, down_ref, other_core(), sent_ref)


def second_half(whole, gain, gate, up, down, sums):
    return call(
        second_kernel,
        [(whole.shape, jnp.bfloat16), ((whole.shape[1], gate.shape[0]), jnp.bfloat16)],
        [whole, gain, gate, up, down, *sums],
        [pltpu.VMEM] * 8,
        limit=30 * MIB,
    )


def final_kernel(stream_ref, came_ref, out_ref):
    total = jnp.sum(came_ref[...].astype(jnp.float32), axis=0)
    out_ref[...] = (stream_ref[...] + total).astype(jnp.bfloat16)


def final_sum(stream, came):
    return call(final_kernel, [(stream.shape, jnp.bfloat16)], [stream, came], [pltpu.VMEM] * 2)[0]


def swap(blocks, axes):
    return lax.all_to_all(blocks, axes, split_axis=0, concat_axis=0, tiled=True)


def other(block):
    return lax.ppermute(block, "c", [(0, 1), (1, 0)])


def per_device(
    queries, k_cache, v_cache, lengths, residual_in, out_weight, norm_gain, gate_weight, up_weight, down_weight
):
    rows = queries.shape[0]
    gain = norm_gain.astype(jnp.float32).reshape(-1, LANES)
    message, weight, residual = attention(lengths, queries, k_cache, v_cache, out_weight, residual_in)
    sent, attended = merge_and_project(swap(message, KV), weight, rows)
    partial = add(own_half(attended, weight), other(sent))
    stream, copies = stream_sum(swap(partial, CHIPS), residual)
    whole = swap(copies, CHIPS)
    sums = first_half(whole, gain, gate_weight, up_weight)
    sent, hidden = second_half(other(whole), gain, gate_weight, up_weight, down_weight, sums)
    partial = add(own_half(hidden, down_weight), other(sent))
    return final_sum(stream, swap(partial, CHIPS))


def solution(mesh):
    fine = Mesh(mesh.devices.reshape(4, 4, 2, 4), ALL)
    placed = (
        P(None, "z", None),
        P(None, KV, "z", None),
        P(None, KV, "z", None),
        P(),
        P(),
        P(("z",) + KV, None),
        P(),
        P(ALL, None),
        P(ALL, None),
        P(ALL, None),
    )
    return jax.shard_map(per_device, mesh=fine, in_specs=placed, out_specs=P(None, ALL), check_vma=False)
```

```python
import functools

import jax
import jax.numpy as jnp
from jax import lax
from jax.experimental import pallas as pl
from jax.experimental.pallas import tpu as pltpu
from jax.sharding import Mesh, PartitionSpec as P

KV = ("x", "y", "c")
ALL = ("x", "y", "c", "z")
CHIPS = ("x", "y", "z")
LANES = 128
MIB = 2**20
LAST = (((1,), (1,)), ((), ()))


def flat_index(axes):
    index = 0
    for axis in axes:
        index = index * lax.axis_size(axis) + lax.axis_index(axis)
    return index


def call(kernel, outs, args, spaces, scratch=(), limit=16 * MIB, flops=0):
    shapes = [jax.ShapeDtypeStruct(*out) for out in outs]
    specs = [pl.BlockSpec(memory_space=pltpu.VMEM)] * len(outs)
    return pl.pallas_call(
        kernel,
        out_shape=shapes,
        in_specs=[pl.BlockSpec(memory_space=space) for space in spaces],
        out_specs=specs,
        scratch_shapes=list(scratch),
        compiler_params=pltpu.CompilerParams(vmem_limit_bytes=limit),
        cost_estimate=pl.CostEstimate(flops=flops, bytes_accessed=MIB, transcendentals=0),
    )(*args)


def attention_kernel(
    groups,
    lengths_hbm,
    q_hbm,
    k_hbm,
    v_hbm,
    residual_hbm,
    weights_ref,
    stats_ref,
    v_ref,
    residual_ref,
    lengths_ref,
    q_ref,
    k_ref,
    sems,
):
    rows, heads, width = q_ref.shape
    slots = k_ref.shape[1]
    span = slots // groups
    size = heads // groups
    columns = pl.ds(pl.multiple_of(flat_index(ALL) * LANES, LANES), LANES)
    loads = [
        pltpu.make_async_copy(source, target, sems.at[i])
        for i, (source, target) in enumerate(
            (
                (q_hbm, q_ref),
                (k_hbm, k_ref),
                (lengths_hbm, lengths_ref),
                (v_hbm, v_ref),
                (residual_hbm.at[:, columns], residual_ref),
            )
        )
    ]
    for load in loads:
        load.start()
    base = flat_index(KV) * span
    head = lax.broadcasted_iota(jnp.int32, (heads, slots), 0)
    slot = lax.broadcasted_iota(jnp.int32, (heads, slots), 1)
    own = (head // size) == (slot % groups)
    position = jnp.where(own, base + slot // groups, jnp.int32(2**30))
    lane = lax.broadcasted_iota(jnp.int32, (heads, width), 1)
    half = width // 2
    for load in loads[:3]:
        load.wait()
    scores = [
        lax.dot_general(q_ref[b], k_ref[b], LAST, preferred_element_type=jnp.float32) * width ** (-0.5)
        for b in range(rows)
    ]
    for b in range(rows):
        live = position < lengths_ref[b]
        masked = jnp.where(live, scores[b], -1e30)
        point = jnp.max(masked, axis=1, keepdims=True).astype(jnp.bfloat16).astype(jnp.float32)
        weight = jnp.where(live, jnp.exp(masked - point), 0.0)
        weights_ref[b] = weight.astype(jnp.bfloat16)
        stats_ref[b] = jnp.where(lane < half // 2, point, jnp.sum(weight, axis=1, keepdims=True))
    for load in loads[3:]:
        load.wait()


def attention(lengths, queries, k_cache, v_cache, residual):
    rows, heads, width = queries.shape
    span, groups = k_cache.shape[1:3]
    cache = (rows, span * groups, width)
    return call(
        functools.partial(attention_kernel, groups),
        [
            ((rows, heads, span * groups), jnp.bfloat16),
            (queries.shape, jnp.float32),
            (cache, jnp.bfloat16),
            ((rows, LANES), jnp.bfloat16),
        ],
        [
            pltpu.with_memory_space_constraint(a, pltpu.HBM)
            for a in (lengths, queries, k_cache.reshape(cache), v_cache.reshape(cache), residual)
        ],
        [pltpu.HBM] * 5,
        [
            pltpu.SMEM(lengths.shape, jnp.int32),
            pltpu.VMEM(queries.shape, jnp.bfloat16),
            pltpu.VMEM(cache, jnp.bfloat16),
            pltpu.SemaphoreType.DMA((5,)),
        ],
        limit=12 * MIB,
    )


def message_kernel(weights_ref, stats_ref, v_ref, message_ref, held):
    rows, heads, _ = weights_ref.shape
    _, height, width = message_ref.shape
    half = width // 2
    lane = lax.broadcasted_iota(jnp.int32, (heads, width), 1)
    outs = [jnp.dot(weights_ref[b], v_ref[b], preferred_element_type=jnp.float32) for b in range(rows)]
    for b in range(rows):
        held[pl.ds(b, heads, stride=height), :] = outs[b]
    for b in range(rows // 2):
        later = pltpu.roll(stats_ref[b + rows // 2], half, 1)
        held[pl.ds(rows + b, heads, stride=height), :] = jnp.where(lane < half, stats_ref[b], later)
    for h in range(heads):
        message_ref[h] = held[h * height : (h + 1) * height, :].astype(jnp.bfloat16)


def message_of(weights, stats, values):
    rows, heads, width = stats.shape
    height = rows + rows // 2
    return call(
        message_kernel,
        [((heads, height, width), jnp.bfloat16)],
        [weights, stats, values],
        [pltpu.VMEM] * 3,
        [pltpu.VMEM((heads * height, width), jnp.float32)],
        limit=8 * MIB,
        flops=10**10,
    )[0]


def columns_of(piece, side, run):
    return pl.ds(pl.multiple_of((2 * piece + side) * run, run), run)


def other_core():
    return 1 - lax.axis_index("c")


def half_product(left, weight_ref, side, out_ref):
    per = lax.axis_size("z")
    run = per * LANES
    for piece in range(out_ref.shape[0] // per):
        product = jnp.dot(left, weight_ref[:, columns_of(piece, side, run)], preferred_element_type=jnp.float32)
        for j in range(per):
            out_ref[piece * per + j] = product[:, j * LANES : (j + 1) * LANES].astype(out_ref.dtype)


def merge_kernel(rows, came_ref, weight_ref, sent_ref, attended_ref):
    width = came_ref.shape[2]
    half = width // 2
    stats = came_ref[:, rows:, :].astype(jnp.float32)
    point = jnp.concatenate([stats[:, :, :1], stats[:, :, half : half + 1]], axis=1)
    quarter = half // 2
    total = jnp.concatenate(
        [stats[:, :, quarter : quarter + 1], stats[:, :, half + quarter : half + quarter + 1]], axis=1
    )
    scale = jnp.exp(point - jnp.max(point, axis=0, keepdims=True))
    out = jnp.sum(scale * came_ref[:, :rows, :].astype(jnp.float32), axis=0)
    attended = (out / jnp.sum(scale * total, axis=0)).astype(jnp.bfloat16)
    attended_ref[...] = attended
    half_product(attended, weight_ref, other_core(), sent_ref)


def merge_and_project(came, weight, rows):
    chips = weight.shape[1] // LANES // 2
    return call(
        functools.partial(merge_kernel, rows),
        [((chips, rows, LANES), jnp.bfloat16), ((rows, came.shape[2]), jnp.bfloat16)],
        [came, weight],
        [pltpu.VMEM] * 2,
        limit=12 * MIB,
        flops=10**10,
    )


def own_kernel(left_ref, weight_ref, out_ref):
    half_product(left_ref[...], weight_ref, lax.axis_index("c"), out_ref)


def own_half(left, weight):
    chips = weight.shape[1] // LANES // 2
    return call(
        own_kernel,
        [((chips, left.shape[0], LANES), jnp.float32)],
        [left, weight],
        [pltpu.VMEM] * 2,
        limit=12 * MIB,
        flops=10**9,
    )[0]


def add_kernel(own_ref, came_ref, out_ref):
    out_ref[...] = (own_ref[...] + came_ref[...].astype(jnp.float32)).astype(jnp.bfloat16)


def add(own, came):
    return call(add_kernel, [(came.shape, jnp.bfloat16)], [own, came], [pltpu.VMEM] * 2)[0]


def stream_kernel(came_ref, residual_ref, stream_ref, sent_ref):
    total = jnp.sum(came_ref[...].astype(jnp.float32), axis=0)
    stream = total + residual_ref[...].astype(jnp.float32)
    stream_ref[...] = stream
    sent_ref[...] = jnp.broadcast_to(stream.astype(jnp.bfloat16)[None], sent_ref.shape)


def stream_sum(came, residual):
    shape = came.shape
    return call(
        stream_kernel,
        [(shape[1:], jnp.float32), (shape, jnp.bfloat16)],
        [came, residual],
        [pltpu.VMEM] * 2,
    )


def gate_up(side, whole_ref, gain_ref, gate_ref, up_ref, gate, up, square):
    per = lax.axis_size("z")
    run = per * LANES
    for piece in range(whole_ref.shape[0] // per):
        parts = []
        for j in range(per):
            part = whole_ref[piece * per + j].astype(jnp.float32)
            square += part * part
            gain = gain_ref[pl.ds((2 * piece + side) * per + j, 1), :]
            parts.append((part * gain).astype(jnp.bfloat16))
        block = jnp.concatenate(parts, axis=1)
        columns = columns_of(piece, side, run)
        gate += lax.dot_general(gate_ref[:, columns], block, LAST, preferred_element_type=jnp.float32)
        up += lax.dot_general(up_ref[:, columns], block, LAST, preferred_element_type=jnp.float32)
    return gate, up, square


def first_kernel(whole_ref, gain_ref, gate_ref, up_ref, gate_out, up_out, square_out):
    zeros = jnp.zeros(gate_out.shape, jnp.float32)
    gate_out[...], up_out[...], square_out[...] = gate_up(
        lax.axis_index("c"), whole_ref, gain_ref, gate_ref, up_ref, zeros, zeros, jnp.zeros(square_out.shape, jnp.float32)
    )


def first_half(whole, gain, gate, up):
    rows, units = whole.shape[1], gate.shape[0]
    return call(
        first_kernel,
        [((units, rows), jnp.float32), ((units, rows), jnp.float32), ((rows, LANES), jnp.float32)],
        [whole, gain, gate, up],
        [pltpu.VMEM] * 4,
        limit=24 * MIB,
        flops=10**9,
    )


def second_kernel(
    whole_ref, gain_ref, gate_ref, up_ref, down_ref, gate_sum, up_sum, square_sum, sent_ref, hidden_ref
):
    gate, up, square = gate_up(
        other_core(), whole_ref, gain_ref, gate_ref, up_ref, gate_sum[...], up_sum[...], square_sum[...]
    )
    width = gate_ref.shape[1]
    factor = lax.rsqrt(jnp.sum(square.T, axis=0, keepdims=True) * (1.0 / width) + 1e-05)
    gate = gate * factor
    hidden = (gate / (1.0 + jnp.exp(-gate)) * (up * factor)).T.astype(jnp.bfloat16)
    hidden_ref[...] = hidden
    half_product(hidden, down_ref, other_core(), sent_ref)


def second_half(whole, gain, gate, up, down, sums):
    return call(
        second_kernel,
        [(whole.shape, jnp.bfloat16), ((whole.shape[1], gate.shape[0]), jnp.bfloat16)],
        [whole, gain, gate, up, down, *sums],
        [pltpu.VMEM] * 8,
        limit=30 * MIB,
    )


def final_kernel(stream_ref, came_ref, out_ref):
    total = jnp.sum(came_ref[...].astype(jnp.float32), axis=0)
    out_ref[...] = (stream_ref[...] + total).astype(jnp.bfloat16)


def final_sum(stream, came):
    return call(final_kernel, [(stream.shape, jnp.bfloat16)], [stream, came], [pltpu.VMEM] * 2)[0]


def swap(blocks, axes):
    return lax.all_to_all(blocks, axes, split_axis=0, concat_axis=0, tiled=True)


def other(block):
    return lax.ppermute(block, "c", [(0, 1), (1, 0)])


def per_device(
    queries, k_cache, v_cache, lengths, residual_in, out_weight, norm_gain, gate_weight, up_weight, down_weight
):
    rows = queries.shape[0]
    gain = norm_gain.astype(jnp.float32).reshape(-1, LANES)
    weights, stats, values, residual = attention(lengths, queries, k_cache, v_cache, residual_in)
    came = swap(message_of(weights, stats, values), KV)
    sent, attended = merge_and_project(came, out_weight, rows)
    partial = add(own_half(attended, out_weight), other(sent))
    stream, copies = stream_sum(swap(partial, CHIPS), residual)
    whole = swap(copies, CHIPS)
    sums = first_half(whole, gain, gate_weight, up_weight)
    sent, hidden = second_half(other(whole), gain, gate_weight, up_weight, down_weight, sums)
    partial = add(own_half(hidden, down_weight), other(sent))
    return final_sum(stream, swap(partial, CHIPS))


def solution(mesh):
    fine = Mesh(mesh.devices.reshape(4, 4, 2, 4), ALL)
    placed = (
        P(None, "z", None),
        P(None, KV, "z", None),
        P(None, KV, "z", None),
        P(),
        P(),
        P(("z",) + KV, None),
        P(),
        P(ALL, None),
        P(ALL, None),
        P(ALL, None),
    )
    return jax.shard_map(per_device, mesh=fine, in_specs=placed, out_specs=P(None, ALL), check_vma=False)
```

```python
import functools

import jax
import jax.numpy as jnp
from jax import lax
from jax.experimental import pallas as pl
from jax.experimental.pallas import tpu as pltpu
from jax.sharding import Mesh, PartitionSpec as P

KV = ("far", "x", "y", "c")
ALL = ("far", "x", "y", "c", "z")
CHIPS = ("far", "x", "y", "z")
NEAR = ("x", "y", "z")
LANES = 128
MIB = 2**20
LAST = (((1,), (1,)), ((), ()))


def flat_index(axes):
    index = 0
    for axis in axes:
        index = index * lax.axis_size(axis) + lax.axis_index(axis)
    return index


def call(kernel, outs, args, spaces, scratch=(), limit=16 * MIB, flops=0):
    shapes = [jax.ShapeDtypeStruct(*out) for out in outs]
    specs = [pl.BlockSpec(memory_space=pltpu.VMEM)] * len(outs)
    return pl.pallas_call(
        kernel,
        out_shape=shapes,
        in_specs=[pl.BlockSpec(memory_space=space) for space in spaces],
        out_specs=specs,
        scratch_shapes=list(scratch),
        compiler_params=pltpu.CompilerParams(vmem_limit_bytes=limit),
        cost_estimate=pl.CostEstimate(flops=flops, bytes_accessed=MIB, transcendentals=0),
    )(*args)


def attention_kernel(
    groups,
    lengths_hbm,
    q_hbm,
    k_hbm,
    v_hbm,
    residual_hbm,
    weights_ref,
    stats_ref,
    v_ref,
    residual_ref,
    lengths_ref,
    q_ref,
    k_ref,
    sems,
):
    rows, heads, width = q_ref.shape
    slots = k_ref.shape[1]
    span = slots // groups
    size = heads // groups
    near = flat_index(("x", "y", "c", "z"))
    distance = lax.axis_size(("x", "y", "c", "z"))
    starts = [pl.multiple_of((near + i * distance) * LANES, LANES) for i in range(lax.axis_size("far"))]
    loads = [
        pltpu.make_async_copy(source, target, sems.at[i])
        for i, (source, target) in enumerate(
            (
                (q_hbm, q_ref),
                (k_hbm, k_ref),
                (lengths_hbm, lengths_ref),
                (v_hbm, v_ref),
                (residual_hbm.at[:, pl.ds(starts[0], LANES)], residual_ref.at[0]),
                (residual_hbm.at[:, pl.ds(starts[1], LANES)], residual_ref.at[1]),
            )
        )
    ]
    for load in loads:
        load.start()
    base = flat_index(KV) * span
    head = lax.broadcasted_iota(jnp.int32, (heads, slots), 0)
    slot = lax.broadcasted_iota(jnp.int32, (heads, slots), 1)
    own = (head // size) == (slot % groups)
    position = jnp.where(own, base + slot // groups, jnp.int32(2**30))
    lane = lax.broadcasted_iota(jnp.int32, (heads, width), 1)
    half = width // 2
    for load in loads[:3]:
        load.wait()
    scores = [
        lax.dot_general(q_ref[b], k_ref[b], LAST, preferred_element_type=jnp.float32) * width ** (-0.5)
        for b in range(rows)
    ]
    for b in range(rows):
        live = position < lengths_ref[b]
        masked = jnp.where(live, scores[b], -1e30)
        point = jnp.max(masked, axis=1, keepdims=True).astype(jnp.bfloat16).astype(jnp.float32)
        weight = jnp.where(live, jnp.exp(masked - point), 0.0)
        weights_ref[b] = weight.astype(jnp.bfloat16)
        stats_ref[b] = jnp.where(lane < half // 2, point, jnp.sum(weight, axis=1, keepdims=True))
    for load in loads[3:]:
        load.wait()


def attention(lengths, queries, k_cache, v_cache, residual):
    rows, heads, width = queries.shape
    span, groups = k_cache.shape[1:3]
    cache = (rows, span * groups, width)
    return call(
        functools.partial(attention_kernel, groups),
        [
            ((rows, heads, span * groups), jnp.bfloat16),
            (queries.shape, jnp.float32),
            (cache, jnp.bfloat16),
            ((2, rows, LANES), jnp.bfloat16),
        ],
        [
            pltpu.with_memory_space_constraint(a, pltpu.HBM)
            for a in (lengths, queries, k_cache.reshape(cache), v_cache.reshape(cache), residual)
        ],
        [pltpu.HBM] * 5,
        [
            pltpu.SMEM(lengths.shape, jnp.int32),
            pltpu.VMEM(queries.shape, jnp.bfloat16),
            pltpu.VMEM(cache, jnp.bfloat16),
            pltpu.SemaphoreType.DMA((6,)),
        ],
        limit=12 * MIB,
    )


def message_kernel(weights_ref, stats_ref, v_ref, message_ref, held):
    rows, heads, _ = weights_ref.shape
    _, height, width = message_ref.shape
    half = width // 2
    lane = lax.broadcasted_iota(jnp.int32, (heads, width), 1)
    outs = [jnp.dot(weights_ref[b], v_ref[b], preferred_element_type=jnp.float32) for b in range(rows)]
    for b in range(rows):
        held[pl.ds(b, heads, stride=height), :] = outs[b]
    for b in range(rows // 2):
        later = pltpu.roll(stats_ref[b + rows // 2], half, 1)
        held[pl.ds(rows + b, heads, stride=height), :] = jnp.where(lane < half, stats_ref[b], later)
    for h in range(heads):
        message_ref[h] = held[h * height : (h + 1) * height, :].astype(jnp.bfloat16)


def message_of(weights, stats, values):
    rows, heads, width = stats.shape
    height = rows + rows // 2
    return call(
        message_kernel,
        [((heads, height, width), jnp.bfloat16)],
        [weights, stats, values],
        [pltpu.VMEM] * 3,
        [pltpu.VMEM((heads * height, width), jnp.float32)],
        limit=8 * MIB,
        flops=10**10,
    )[0]


def columns_of(piece, side, run):
    return pl.ds(pl.multiple_of((2 * piece + side) * run, run), run)


def other_core():
    return 1 - lax.axis_index("c")


def half_product(left, weight_ref, side, out_ref, paired):
    per = lax.axis_size("z")
    run = per * LANES
    places = out_ref.shape[0] // per
    halves = lax.axis_size("far")
    for piece in range(places):
        product = jnp.dot(left, weight_ref[:, columns_of(piece, side, run)], preferred_element_type=jnp.float32)
        half, near = divmod(piece, places // halves)
        for j in range(per):
            at = (near * per + j) * halves + half if paired else piece * per + j
            out_ref[at] = product[:, j * LANES : (j + 1) * LANES].astype(out_ref.dtype)


def merge_kernel(rows, came_ref, weight_ref, sent_ref, attended_ref):
    width = came_ref.shape[2]
    half = width // 2
    stats = came_ref[:, rows:, :].astype(jnp.float32)
    point = jnp.concatenate([stats[:, :, :1], stats[:, :, half : half + 1]], axis=1)
    quarter = half // 2
    total = jnp.concatenate(
        [stats[:, :, quarter : quarter + 1], stats[:, :, half + quarter : half + quarter + 1]], axis=1
    )
    scale = jnp.exp(point - jnp.max(point, axis=0, keepdims=True))
    out = jnp.sum(scale * came_ref[:, :rows, :].astype(jnp.float32), axis=0)
    attended = (out / jnp.sum(scale * total, axis=0)).astype(jnp.bfloat16)
    attended_ref[...] = attended
    half_product(attended, weight_ref, other_core(), sent_ref, True)


def merge_and_project(came, weight, rows):
    chips = weight.shape[1] // LANES // 2
    return call(
        functools.partial(merge_kernel, rows),
        [((chips, rows, LANES), jnp.bfloat16), ((rows, came.shape[2]), jnp.bfloat16)],
        [came, weight],
        [pltpu.VMEM] * 2,
        limit=12 * MIB,
        flops=10**10,
    )


def own_kernel(paired, left_ref, weight_ref, out_ref):
    half_product(left_ref[...], weight_ref, lax.axis_index("c"), out_ref, paired)


def own_half(left, weight, paired):
    chips = weight.shape[1] // LANES // 2
    return call(
        functools.partial(own_kernel, paired),
        [((chips, left.shape[0], LANES), jnp.float32)],
        [left, weight],
        [pltpu.VMEM] * 2,
        limit=12 * MIB,
        flops=10**9,
    )[0]


def add_kernel(own_ref, came_ref, out_ref):
    out_ref[...] = (own_ref[...] + came_ref[...].astype(jnp.float32)).astype(jnp.bfloat16)


def add(own, came):
    return call(add_kernel, [(came.shape, jnp.bfloat16)], [own, came], [pltpu.VMEM] * 2)[0]


def stream_kernel(came_ref, residual_ref, sent_ref):
    total = jnp.sum(came_ref[...].astype(jnp.float32), axis=0)
    residual = residual_ref[...].astype(jnp.float32)
    total += jnp.where(lax.axis_index("far") == 0, residual, 0.0)
    sent_ref[...] = jnp.broadcast_to(total.astype(jnp.bfloat16)[None], sent_ref.shape)


def stream_sum(came, residual):
    chips = lax.axis_size(CHIPS)
    return call(
        stream_kernel,
        [((chips, *residual.shape), jnp.bfloat16)],
        [came, residual],
        [pltpu.VMEM] * 2,
    )[0]


def stream_block(whole_ref, near, half):
    chips = whole_ref.shape[0] // lax.axis_size("far")
    return whole_ref[near, half].astype(jnp.float32) + whole_ref[chips + near, half].astype(jnp.float32)


def gate_up(side, whole_ref, gain_ref, gate_ref, up_ref, gate, up, square):
    per = lax.axis_size("z")
    run = per * LANES
    places = whole_ref.shape[0] // per
    for piece in range(places):
        half, near = divmod(piece, places // lax.axis_size("far"))
        parts = []
        for j in range(per):
            part = stream_block(whole_ref, near * per + j, half)
            square += part * part
            gain = gain_ref[pl.ds((2 * piece + side) * per + j, 1), :]
            parts.append((part * gain).astype(jnp.bfloat16))
        block = jnp.concatenate(parts, axis=1)
        columns = columns_of(piece, side, run)
        gate += lax.dot_general(gate_ref[:, columns], block, LAST, preferred_element_type=jnp.float32)
        up += lax.dot_general(up_ref[:, columns], block, LAST, preferred_element_type=jnp.float32)
    return gate, up, square


def first_kernel(whole_ref, gain_ref, gate_ref, up_ref, gate_out, up_out, square_out, stream_out):
    zeros = jnp.zeros(gate_out.shape, jnp.float32)
    gate_out[...], up_out[...], square_out[...] = gate_up(
        lax.axis_index("c"), whole_ref, gain_ref, gate_ref, up_ref, zeros, zeros, jnp.zeros(square_out.shape, jnp.float32)
    )
    stream_out[...] = stream_block(whole_ref, flat_index(NEAR), lax.axis_index("far"))


def first_half(whole, gain, gate, up):
    rows, units = whole.shape[2], gate.shape[0]
    return call(
        first_kernel,
        [((units, rows), jnp.float32)] * 2 + [((rows, LANES), jnp.float32)] * 2,
        [whole, gain, gate, up],
        [pltpu.VMEM] * 4,
        limit=24 * MIB,
        flops=10**9,
    )


def second_kernel(
    whole_ref, gain_ref, gate_ref, up_ref, down_ref, gate_sum, up_sum, square_sum, sent_ref, hidden_ref
):
    gate, up, square = gate_up(
        other_core(), whole_ref, gain_ref, gate_ref, up_ref, gate_sum[...], up_sum[...], square_sum[...]
    )
    width = gate_ref.shape[1]
    factor = lax.rsqrt(jnp.sum(square.T, axis=0, keepdims=True) * (1.0 / width) + 1e-05)
    gate = gate * factor
    hidden = (gate / (1.0 + jnp.exp(-gate)) * (up * factor)).T.astype(jnp.bfloat16)
    hidden_ref[...] = hidden
    half_product(hidden, down_ref, other_core(), sent_ref, False)


def second_half(whole, gain, gate, up, down, sums):
    return call(
        second_kernel,
        [((whole.shape[0], *whole.shape[2:]), jnp.bfloat16), ((whole.shape[2], gate.shape[0]), jnp.bfloat16)],
        [whole, gain, gate, up, down, *sums],
        [pltpu.VMEM] * 8,
        limit=30 * MIB,
    )


def final_kernel(stream_ref, came_ref, out_ref):
    total = jnp.sum(came_ref[...].astype(jnp.float32), axis=0)
    out_ref[...] = (stream_ref[...] + total).astype(jnp.bfloat16)


def final_sum(stream, came):
    return call(final_kernel, [(stream.shape, jnp.bfloat16)], [stream, came], [pltpu.VMEM] * 2)[0]


def swap(blocks, axes):
    return lax.all_to_all(blocks, axes, split_axis=0, concat_axis=0, tiled=True)


def other(block):
    return lax.ppermute(block, "c", [(0, 1), (1, 0)])


def per_device(
    queries, k_cache, v_cache, lengths, residual_in, out_weight, norm_gain, gate_weight, up_weight, down_weight
):
    rows = queries.shape[0]
    gain = norm_gain.astype(jnp.float32).reshape(-1, LANES)
    weights, stats, values, residual = attention(lengths, queries, k_cache, v_cache, residual_in)
    came = swap(message_of(weights, stats, values), KV)
    sent, attended = merge_and_project(came, out_weight, rows)
    partial = add(own_half(attended, out_weight, True), other(sent))
    near = lax.axis_size(NEAR)
    partial = swap(partial.reshape(near, -1, rows, LANES), NEAR)
    whole = swap(stream_sum(partial, residual), CHIPS)
    *sums, stream = first_half(whole, gain, gate_weight, up_weight)
    sent, hidden = second_half(other(whole), gain, gate_weight, up_weight, down_weight, sums)
    partial = add(own_half(hidden, down_weight, False), other(sent))
    return final_sum(stream, swap(partial, CHIPS))


def solution(mesh):
    fine = Mesh(mesh.devices.reshape(2, 2, 4, 2, 4), ALL)
    placed = (
        P(None, "z", None),
        P(None, KV, "z", None),
        P(None, KV, "z", None),
        P(),
        P(),
        P(("z",) + KV, None),
        P(),
        P(ALL, None),
        P(ALL, None),
        P(ALL, None),
    )
    return jax.shard_map(per_device, mesh=fine, in_specs=placed, out_specs=P(None, ALL), check_vma=False)
```

```python
import functools

import jax
import jax.numpy as jnp
from jax import lax
from jax.experimental import pallas as pl
from jax.experimental.pallas import tpu as pltpu
from jax.sharding import Mesh, PartitionSpec as P

KV = ("x", "far", "y", "c")
ALL = ("x", "far", "y", "c", "z")
PLACES = ("x", "far", "y", "z")
CHIPS = ("far", "x", "y", "z")
NEAR = ("x", "y", "z")
LANES = 128
MIB = 2**20
LAST = (((1,), (1,)), ((), ()))


def flat_index(axes):
    index = 0
    for axis in axes:
        index = index * lax.axis_size(axis) + lax.axis_index(axis)
    return index


def call(kernel, outs, args, spaces, scratch=(), limit=16 * MIB, flops=0):
    shapes = [jax.ShapeDtypeStruct(*out) for out in outs]
    specs = [pl.BlockSpec(memory_space=pltpu.VMEM)] * len(outs)
    return pl.pallas_call(
        kernel,
        out_shape=shapes,
        in_specs=[pl.BlockSpec(memory_space=space) for space in spaces],
        out_specs=specs,
        scratch_shapes=list(scratch),
        compiler_params=pltpu.CompilerParams(vmem_limit_bytes=limit),
        cost_estimate=pl.CostEstimate(flops=flops, bytes_accessed=MIB, transcendentals=0),
    )(*args)


def attention_kernel(
    groups,
    lengths_hbm,
    q_hbm,
    k_hbm,
    v_hbm,
    residual_hbm,
    weights_ref,
    stats_ref,
    v_ref,
    residual_ref,
    lengths_ref,
    q_ref,
    k_ref,
    sems,
):
    rows, heads, width = q_ref.shape
    slots = k_ref.shape[1]
    span = slots // groups
    size = heads // groups
    distance = lax.axis_size(("y", "c", "z"))
    near = flat_index(ALL) - lax.axis_index("far") * distance
    starts = [pl.multiple_of((near + i * distance) * LANES, LANES) for i in range(lax.axis_size("far"))]
    loads = [
        pltpu.make_async_copy(source, target, sems.at[i])
        for i, (source, target) in enumerate(
            (
                (q_hbm, q_ref),
                (k_hbm, k_ref),
                (lengths_hbm, lengths_ref),
                (v_hbm, v_ref),
                (residual_hbm.at[:, pl.ds(starts[0], LANES)], residual_ref.at[0]),
                (residual_hbm.at[:, pl.ds(starts[1], LANES)], residual_ref.at[1]),
            )
        )
    ]
    for load in loads:
        load.start()
    base = flat_index(KV) * span
    head = lax.broadcasted_iota(jnp.int32, (heads, slots), 0)
    slot = lax.broadcasted_iota(jnp.int32, (heads, slots), 1)
    own = (head // size) == (slot % groups)
    position = jnp.where(own, base + slot // groups, jnp.int32(2**30))
    lane = lax.broadcasted_iota(jnp.int32, (heads, width), 1)
    half = width // 2
    for load in loads[:3]:
        load.wait()
    scores = [
        lax.dot_general(q_ref[b], k_ref[b], LAST, preferred_element_type=jnp.float32) * width ** (-0.5)
        for b in range(rows)
    ]
    for b in range(rows):
        live = position < lengths_ref[b]
        masked = jnp.where(live, scores[b], -1e30)
        point = jnp.max(masked, axis=1, keepdims=True).astype(jnp.bfloat16).astype(jnp.float32)
        weight = jnp.where(live, jnp.exp(masked - point), 0.0)
        weights_ref[b] = weight.astype(jnp.bfloat16)
        stats_ref[b] = jnp.where(lane < half // 2, point, jnp.sum(weight, axis=1, keepdims=True))
    for load in loads[3:]:
        load.wait()


def attention(lengths, queries, k_cache, v_cache, residual):
    rows, heads, width = queries.shape
    span, groups = k_cache.shape[1:3]
    cache = (rows, span * groups, width)
    return call(
        functools.partial(attention_kernel, groups),
        [
            ((rows, heads, span * groups), jnp.bfloat16),
            (queries.shape, jnp.float32),
            (cache, jnp.bfloat16),
            ((2, rows, LANES), jnp.bfloat16),
        ],
        [
            pltpu.with_memory_space_constraint(a, pltpu.HBM)
            for a in (lengths, queries, k_cache.reshape(cache), v_cache.reshape(cache), residual)
        ],
        [pltpu.HBM] * 5,
        [
            pltpu.SMEM(lengths.shape, jnp.int32),
            pltpu.VMEM(queries.shape, jnp.bfloat16),
            pltpu.VMEM(cache, jnp.bfloat16),
            pltpu.SemaphoreType.DMA((6,)),
        ],
        limit=12 * MIB,
    )


def message_kernel(weights_ref, stats_ref, v_ref, message_ref, held):
    rows, heads, _ = weights_ref.shape
    _, height, width = message_ref.shape
    half = width // 2
    lane = lax.broadcasted_iota(jnp.int32, (heads, width), 1)
    outs = [jnp.dot(weights_ref[b], v_ref[b], preferred_element_type=jnp.float32) for b in range(rows)]
    for b in range(rows):
        held[pl.ds(b, heads, stride=height), :] = outs[b]
    for b in range(rows // 2):
        later = pltpu.roll(stats_ref[b + rows // 2], half, 1)
        held[pl.ds(rows + b, heads, stride=height), :] = jnp.where(lane < half, stats_ref[b], later)
    for h in range(heads):
        message_ref[h] = held[h * height : (h + 1) * height, :].astype(jnp.bfloat16)


def message_of(weights, stats, values):
    rows, heads, width = stats.shape
    height = rows + rows // 2
    return call(
        message_kernel,
        [((heads, height, width), jnp.bfloat16)],
        [weights, stats, values],
        [pltpu.VMEM] * 3,
        [pltpu.VMEM((heads * height, width), jnp.float32)],
        limit=8 * MIB,
        flops=10**10,
    )[0]


def columns_of(piece, side, run):
    return pl.ds(pl.multiple_of((2 * piece + side) * run, run), run)


def other_core():
    return 1 - lax.axis_index("c")


def half_and_near(piece):
    size = lax.axis_size("y")
    row, inside = divmod(piece, size * lax.axis_size("far"))
    half, y = divmod(inside, size)
    return half, row * size + y


def half_product(left, weight_ref, side, out_ref, paired):
    per = lax.axis_size("z")
    run = per * LANES
    places = out_ref.shape[0] // per
    halves = lax.axis_size("far")
    for piece in range(places):
        product = jnp.dot(left, weight_ref[:, columns_of(piece, side, run)], preferred_element_type=jnp.float32)
        half, near = half_and_near(piece)
        for j in range(per):
            at = (near * per + j) * halves + half if paired else piece * per + j
            out_ref[at] = product[:, j * LANES : (j + 1) * LANES].astype(out_ref.dtype)


def merge_kernel(rows, came_ref, weight_ref, sent_ref, attended_ref):
    width = came_ref.shape[2]
    half = width // 2
    stats = came_ref[:, rows:, :].astype(jnp.float32)
    point = jnp.concatenate([stats[:, :, :1], stats[:, :, half : half + 1]], axis=1)
    quarter = half // 2
    total = jnp.concatenate(
        [stats[:, :, quarter : quarter + 1], stats[:, :, half + quarter : half + quarter + 1]], axis=1
    )
    scale = jnp.exp(point - jnp.max(point, axis=0, keepdims=True))
    out = jnp.sum(scale * came_ref[:, :rows, :].astype(jnp.float32), axis=0)
    attended = (out / jnp.sum(scale * total, axis=0)).astype(jnp.bfloat16)
    attended_ref[...] = attended
    half_product(attended, weight_ref, other_core(), sent_ref, True)


def merge_and_project(came, weight, rows):
    chips = weight.shape[1] // LANES // 2
    return call(
        functools.partial(merge_kernel, rows),
        [((chips, rows, LANES), jnp.bfloat16), ((rows, came.shape[2]), jnp.bfloat16)],
        [came, weight],
        [pltpu.VMEM] * 2,
        limit=12 * MIB,
        flops=10**10,
    )


def own_kernel(paired, left_ref, weight_ref, out_ref):
    half_product(left_ref[...], weight_ref, lax.axis_index("c"), out_ref, paired)


def own_half(left, weight, paired):
    chips = weight.shape[1] // LANES // 2
    return call(
        functools.partial(own_kernel, paired),
        [((chips, left.shape[0], LANES), jnp.float32)],
        [left, weight],
        [pltpu.VMEM] * 2,
        limit=12 * MIB,
        flops=10**9,
    )[0]


def add_kernel(own_ref, came_ref, out_ref):
    out_ref[...] = (own_ref[...] + came_ref[...].astype(jnp.float32)).astype(jnp.bfloat16)


def add(own, came):
    return call(add_kernel, [(came.shape, jnp.bfloat16)], [own, came], [pltpu.VMEM] * 2)[0]


def stream_kernel(came_ref, residual_ref, sent_ref):
    total = jnp.sum(came_ref[...].astype(jnp.float32), axis=0)
    residual = residual_ref[...].astype(jnp.float32)
    total += jnp.where(lax.axis_index("far") == 0, residual, 0.0)
    sent_ref[...] = jnp.broadcast_to(total.astype(jnp.bfloat16)[None], sent_ref.shape)


def stream_sum(came, residual):
    chips = lax.axis_size(CHIPS)
    return call(
        stream_kernel,
        [((chips, *residual.shape), jnp.bfloat16)],
        [came, residual],
        [pltpu.VMEM] * 2,
    )[0]


def stream_block(whole_ref, near, half):
    chips = whole_ref.shape[0] // lax.axis_size("far")
    return whole_ref[near, half].astype(jnp.float32) + whole_ref[chips + near, half].astype(jnp.float32)


def gate_up(side, whole_ref, gain_ref, gate_ref, up_ref, gate, up, square):
    per = lax.axis_size("z")
    run = per * LANES
    for piece in range(whole_ref.shape[0] // per):
        half, near = half_and_near(piece)
        parts = []
        for j in range(per):
            part = stream_block(whole_ref, near * per + j, half)
            square += part * part
            gain = gain_ref[pl.ds((2 * piece + side) * per + j, 1), :]
            parts.append((part * gain).astype(jnp.bfloat16))
        block = jnp.concatenate(parts, axis=1)
        columns = columns_of(piece, side, run)
        gate += lax.dot_general(gate_ref[:, columns], block, LAST, preferred_element_type=jnp.float32)
        up += lax.dot_general(up_ref[:, columns], block, LAST, preferred_element_type=jnp.float32)
    return gate, up, square


def first_kernel(whole_ref, gain_ref, gate_ref, up_ref, gate_out, up_out, square_out, stream_out):
    zeros = jnp.zeros(gate_out.shape, jnp.float32)
    gate_out[...], up_out[...], square_out[...] = gate_up(
        lax.axis_index("c"), whole_ref, gain_ref, gate_ref, up_ref, zeros, zeros, jnp.zeros(square_out.shape, jnp.float32)
    )
    stream_out[...] = stream_block(whole_ref, flat_index(NEAR), lax.axis_index("far"))


def first_half(whole, gain, gate, up):
    rows, units = whole.shape[2], gate.shape[0]
    return call(
        first_kernel,
        [((units, rows), jnp.float32)] * 2 + [((rows, LANES), jnp.float32)] * 2,
        [whole, gain, gate, up],
        [pltpu.VMEM] * 4,
        limit=24 * MIB,
        flops=10**9,
    )


def second_kernel(
    whole_ref, gain_ref, gate_ref, up_ref, down_ref, gate_sum, up_sum, square_sum, sent_ref, hidden_ref
):
    gate, up, square = gate_up(
        other_core(), whole_ref, gain_ref, gate_ref, up_ref, gate_sum[...], up_sum[...], square_sum[...]
    )
    width = gate_ref.shape[1]
    factor = lax.rsqrt(jnp.sum(square.T, axis=0, keepdims=True) * (1.0 / width) + 1e-05)
    gate = gate * factor
    hidden = (gate / (1.0 + jnp.exp(-gate)) * (up * factor)).T.astype(jnp.bfloat16)
    hidden_ref[...] = hidden
    half_product(hidden, down_ref, other_core(), sent_ref, False)


def second_half(whole, gain, gate, up, down, sums):
    return call(
        second_kernel,
        [((whole.shape[0], *whole.shape[2:]), jnp.bfloat16), ((whole.shape[2], gate.shape[0]), jnp.bfloat16)],
        [whole, gain, gate, up, down, *sums],
        [pltpu.VMEM] * 8,
        limit=30 * MIB,
    )


def final_kernel(stream_ref, came_ref, out_ref):
    total = jnp.sum(came_ref[...].astype(jnp.float32), axis=0)
    out_ref[...] = (stream_ref[...] + total).astype(jnp.bfloat16)


def final_sum(stream, came):
    return call(final_kernel, [(stream.shape, jnp.bfloat16)], [stream, came], [pltpu.VMEM] * 2)[0]


def swap(blocks, axes):
    return lax.all_to_all(blocks, axes, split_axis=0, concat_axis=0, tiled=True)


def other(block):
    return lax.ppermute(block, "c", [(0, 1), (1, 0)])


def per_device(
    queries, k_cache, v_cache, lengths, residual_in, out_weight, norm_gain, gate_weight, up_weight, down_weight
):
    rows = queries.shape[0]
    gain = norm_gain.astype(jnp.float32).reshape(-1, LANES)
    weights, stats, values, residual = attention(lengths, queries, k_cache, v_cache, residual_in)
    came = swap(message_of(weights, stats, values), KV)
    sent, attended = merge_and_project(came, out_weight, rows)
    partial = add(own_half(attended, out_weight, True), other(sent))
    near = lax.axis_size(NEAR)
    partial = swap(partial.reshape(near, -1, rows, LANES), NEAR)
    whole = swap(stream_sum(partial, residual), CHIPS)
    *sums, stream = first_half(whole, gain, gate_weight, up_weight)
    sent, hidden = second_half(other(whole), gain, gate_weight, up_weight, down_weight, sums)
    partial = add(own_half(hidden, down_weight, False), other(sent))
    return final_sum(stream, swap(partial, PLACES))


def solution(mesh):
    fine = Mesh(mesh.devices.reshape(4, 2, 2, 2, 4), ALL)
    placed = (
        P(None, "z", None),
        P(None, KV, "z", None),
        P(None, KV, "z", None),
        P(),
        P(),
        P(("z",) + KV, None),
        P(),
        P(ALL, None),
        P(ALL, None),
        P(ALL, None),
    )
    return jax.shard_map(per_device, mesh=fine, in_specs=placed, out_specs=P(None, ALL), check_vma=False)
```
